256 devices in a mesh: section: 2 (over z_lo), dp: 4 (over y), tensor: 32 (over x, z_hi, core).
Axes of the slice: x: 4, y: 4, z: 8 (z_hi: 4, z_lo: 2; z = z_hi * 2 + z_lo), core: 2. Of those that a mesh axis runs over, the one named last changes fastest.
Arguments:
- inputs: bfloat16 [2, 2048, 8192], P('section', 'dp', 'tensor'), may hold values from -6 to 6
- cotangent: bfloat16 [2, 2048, 16384], P('section', 'dp', 'tensor'), may hold values from -6 to 6
- weight: bfloat16 [2, 8192, 16384], P('section', 'tensor'), may hold values from -0.0625 to 0.0625
- params: float32 [2, 4, 8192, 256], P('section', None, 'tensor'), may hold values from -0.08 to 0.08
- perms: int32 [2, 4, 8192], P('section', None, 'tensor'), may hold values from 0 to 8191, as said below
- resid_top: bfloat16 [2048, 8192], P('dp', 'tensor'), may hold values from -6 to 6
Outputs:
- resid_grad: bfloat16 [2, 2048, 8192], P('section', 'dp', 'tensor')
- param_grad: float32 [2, 4, 8192, 256], P('section', None, 'tensor')
The draws below stay inside these ranges and needn't reach their ends.
Inputs may be any that keep to these rules, and one draw needn't show every extreme that they name: perms[s, k] is a permutation of the 8192 rows; it sends each row to a row of the same group, where the group of row block b (blocks of 256 rows) is blocks b and b XOR (8192 // (256 * 2**(k + 1))), k counted from 0.
All inputs are finite; a program needn't handle non-finite values.
Results may differ from the reference program's by a relative error of at most 0.0076.
Values may be sent and summed in bfloat16 or wider, within the bound.
No kernel may reach another device: no remote copies, remote signals or barrier semaphores. Data moves between devices by JAX's collectives and lax.ppermute only.
A program may use at most 128 MiB of HBM per device.

```python
import jax
import jax.numpy as jnp
from jax import lax

D = 8192
FF = 16384
BLOCK = 256
FACTORS = 4
TOKENS = 2048
SECTIONS = 2


def draw_perms(key, part):
    key = jax.random.fold_in(key, 11)
    count = D // BLOCK
    layers = []
    for section in range(SECTIONS):
        factor_rows = []
        for factor in range(FACTORS):
            stride = count >> factor + 1
            upper = count // (2 * stride)
            keys = jax.random.split(jax.random.fold_in(key, section * FACTORS + factor), upper * stride)
            member = jax.vmap(lambda single: jax.random.permutation(single, 2 * BLOCK))(keys)
            member = member.reshape(upper, stride, 2, BLOCK).astype(jnp.int32)
            high_index = jnp.arange(upper, dtype=jnp.int32)[:, None, None, None]
            low_index = jnp.arange(stride, dtype=jnp.int32)[None, :, None, None]
            source = ((high_index * 2 + member // BLOCK) * stride + low_index) * BLOCK + member % BLOCK
            factor_rows.append(jnp.transpose(source, (0, 2, 1, 3)).reshape(D))
        layers.append(jnp.stack(factor_rows))
    return jnp.stack(layers).astype(jnp.int32)


def steps_of(key, shape, pieces, least, high):
    factor_of, own = 1.0, jax.random.fold_in(key, 6)
    for position, shards_of in pieces:
        draws = jnp.exp(jax.random.uniform(jax.random.fold_in(own, position), (shards_of,), jnp.float32, least / len(pieces), high / len(pieces)))
        factor_of = factor_of * jnp.repeat(draws, shape[position] // shards_of).reshape([-1 if axis == position else 1 for axis in range(len(shape))])
    return factor_of


def normal_values(rng, extent, scale, bound, cuts=(), kind=jnp.bfloat16):
    result = jax.random.normal(rng, extent, jnp.float32) * scale
    if len(cuts) > 0:
        result = steps_of(rng, extent, cuts, -0.22, 0.18) * result
    return jnp.clip(result, min=-bound, max=bound).astype(kind)


def setup_inputs(seed: int = 0) -> dict:
    key_list = jax.random.split(jax.random.key(seed), 7)
    return {
        "inputs": normal_values(key_list[0], (SECTIONS, TOKENS, D), 1.0, 6.0, ((0, 2), (1, 4), (2, 32))),
        "cotangent": normal_values(key_list[1], (SECTIONS, TOKENS, FF), 1.0, 6.0, ((0, 2), (1, 4), (2, 32))),
        "weight": normal_values(key_list[2], (SECTIONS, D, FF), D ** -0.5, 0.0625, ((0, 2), (1, 32))),
        "params": normal_values(key_list[3], (SECTIONS, FACTORS, D, BLOCK), 0.012, 0.08, ((0, 2), (2, 32)), jnp.float32),
        "perms": draw_perms(jax.random.fold_in(key_list[6], 71), 0),
        "resid_top": normal_values(key_list[5], (TOKENS, D), 1.0, 6.0, ((0, 4), (1, 32))),
    }


def cayley(blocks):
    highest = lax.Precision.HIGHEST
    skew = blocks - jnp.swapaxes(blocks, -1, -2)
    eye = jnp.eye(blocks.shape[-1], dtype=jnp.float32)
    square = jnp.matmul(skew, skew, precision=highest)
    plus = eye + skew
    numer = jnp.matmul(plus, plus, precision=highest)
    lower = jnp.linalg.cholesky(eye - square)
    half = jax.scipy.linalg.solve_triangular(lower, numer, lower=True)
    trans_rot = jax.scipy.linalg.solve_triangular(lower, half, lower=True, trans=1)
    return jnp.swapaxes(trans_rot, -1, -2)

def turn(values, rotation):
    shaped = values.astype(jnp.float32).reshape(values.shape[0], -1, BLOCK)
    return jnp.einsum('tbi,bij->tbj', shaped, rotation.astype(jnp.float32)).reshape(values.shape)

def turn_back(values, rotation):
    shaped = values.astype(jnp.float32).reshape(values.shape[0], -1, BLOCK)
    return jnp.einsum('tbi,bji->tbj', shaped, rotation.astype(jnp.float32)).reshape(values.shape)

def reference(inputs, cotangent, weight, params, perms, resid_top):
    count = D // BLOCK
    layer_dx = []
    grads = []
    for section in range(SECTIONS):
        blocks = params[section].reshape(FACTORS, count, BLOCK, BLOCK)
        rot, pullback = jax.vjp(cayley, blocks)
        rounded = rot.astype(jnp.bfloat16)
        chain = [None] * FACTORS
        chain[FACTORS - 1] = inputs[section]
        for factor in range(FACTORS - 1, 0, -1):
            moved = turn(chain[factor], rounded[factor]).astype(jnp.bfloat16)
            chain[factor - 1] = jnp.zeros_like(moved).at[:, perms[section, factor]].set(moved)
        plain = lax.dot_general(cotangent[section].astype(jnp.float32), weight[section].astype(jnp.float32), (((1,), (1,)), ((), ())), preferred_element_type=jnp.float32).astype(jnp.bfloat16)
        back = plain[:, perms[section, 0]]
        drot = []
        for factor in range(FACTORS):
            left = chain[factor].astype(jnp.float32).reshape(-1, count, BLOCK)
            right = back.astype(jnp.float32).reshape(-1, count, BLOCK)
            drot.append(jnp.einsum('tbi,tbj->bij', left, right) / jnp.sqrt(jnp.float32(TOKENS)))
            turned = turn_back(back, rounded[factor])
            if factor + 1 < FACTORS:
                back = turned.astype(jnp.bfloat16)[:, perms[section, factor + 1]]
        layer_dx.append(turned)
        grads.append(pullback(jnp.stack(drot))[0].reshape(FACTORS, D, BLOCK))
    total = resid_top.astype(jnp.float32)
    outputs = [None] * SECTIONS
    for section in range(SECTIONS - 1, -1, -1):
        total = total + layer_dx[section]
        outputs[section] = total.astype(jnp.bfloat16)
    return (jnp.stack(outputs), jnp.stack(grads))
```

```python
import functools
import math

import jax
import jax.numpy as jnp
from jax import lax
from jax.experimental import pallas as pl
from jax.experimental.pallas import tpu as pltpu
from jax.sharding import PartitionSpec as P

BLOCK = 256
FACTORS = 4
HALF = BLOCK // 2
REPLICAS = 4
SPLIT = 2
XS, ZS, CS = 4, 4, 2
F32, BF16 = jnp.float32, jnp.bfloat16
HIGHEST = lax.Precision.HIGHEST
PAIR_BITS = (16, 8, 4, 2)


def params_for(limit):
    return pltpu.CompilerParams(vmem_limit_bytes=limit << 20)


def whole():
    return pl.BlockSpec(memory_space=pltpu.VMEM)


def cost(flops, moved):
    return pl.CostEstimate(flops=flops, bytes_accessed=moved, transcendentals=0)


def identity():
    rows = lax.broadcasted_iota(jnp.int32, (BLOCK, BLOCK), 0)
    cols = lax.broadcasted_iota(jnp.int32, (BLOCK, BLOCK), 1)
    return (rows == cols).astype(F32)


def low_dot(left, right):
    return jnp.dot(left.astype(BF16), right.astype(BF16), preferred_element_type=F32)


def high_dot(left, right):
    return jnp.dot(left, right, preferred_element_type=F32, precision=HIGHEST)


def cayley_kernel(a_ref, rot_ref, q_ref, s_ref):
    eye = identity()
    for k in range(FACTORS):
        a = a_ref[k]
        skew = a - a.T
        s_ref[k] = skew
        square = low_dot(skew, skew)
        row = jnp.max(jnp.sum(jnp.abs(skew), axis=1))
        row_square = jnp.max(jnp.sum(jnp.abs(square), axis=1))
        top = 1.0 + 1.1 * jnp.minimum(row_square, row * row)
        q_ref[k] = (2.0 / (1.0 + top)) * (eye - skew)

    def phase(dot, limit, most):
        def more(carry):
            return (carry[0] < most) & (carry[1] > limit)

        def step(carry):
            worst = jnp.float32(0)
            errors = []
            for k in range(FACTORS):
                error = eye - (q_ref[k] + dot(s_ref[k], q_ref[k]))
                errors.append(error)
                worst = jnp.maximum(worst, jnp.sum(error * error))
            for k in range(FACTORS):
                q_ref[k] = q_ref[k] + low_dot(q_ref[k], errors[k])
            return carry[0] + 1, worst

        lax.while_loop(more, step, (jnp.int32(0), jnp.float32(3e38)))

    phase(low_dot, 0.25, 24)
    phase(high_dot, 1e-6, 12)
    for k in range(FACTORS):
        rot_ref[k] = (2.0 * q_ref[k] - eye).astype(BF16)


def cayley(blocks):
    shape = (FACTORS, BLOCK, BLOCK)
    return pl.pallas_call(
        cayley_kernel,
        out_shape=(jax.ShapeDtypeStruct(shape, BF16), jax.ShapeDtypeStruct(shape, F32)),
        in_specs=[whole()],
        out_specs=(whole(), whole()),
        scratch_shapes=[pltpu.VMEM(shape, F32)],
        compiler_params=params_for(24),
        cost_estimate=cost(7 * 10**9, 10 * FACTORS * BLOCK * BLOCK),
        name="cayley",
    )(blocks)


def triangle(lower):
    rows = lax.broadcasted_iota(jnp.int32, (HALF, HALF), 0)
    cols = lax.broadcasted_iota(jnp.int32, (HALF, HALF), 1)
    return rows > cols if lower else rows < cols


def pull_kernel(first, count, scale, place_ref, *refs):
    drots, (q_ref,), outs, (packed,) = refs[:count], refs[count : count + 1], refs[-5:-1], refs[-1:]
    share = HALF // len(outs)
    for k in range(count):
        q_t = q_ref[first + k].T
        grad = high_dot(high_dot(q_t, drots[k][...]), q_t) * (-2.0 * scale)
        grad = grad - grad.T
        packed[k, :, :HALF] = jnp.where(
            triangle(True), grad[HALF:, HALF:], grad[:HALF, :HALF]
        )
        packed[k, :, HALF:] = grad[:HALF, HALF:]
    for ahead, out_ref in enumerate(outs):
        start = pl.multiple_of(lax.rem(place_ref[0] + ahead, len(outs)) * share, share)
        out_ref[...] = packed[:, pl.ds(start, share), :]


def pull(place, drots, q, first, scale):
    count = len(drots)
    shape = jax.ShapeDtypeStruct((count, HALF // REPLICAS, BLOCK), F32)
    return pl.pallas_call(
        functools.partial(pull_kernel, first, count, scale),
        grid_spec=pltpu.PrefetchScalarGridSpec(
            num_scalar_prefetch=1,
            grid=(1,),
            in_specs=[whole()] * (count + 1),
            out_specs=[whole()] * REPLICAS,
            scratch_shapes=[pltpu.VMEM((count, HALF, BLOCK), F32)],
        ),
        out_shape=[shape] * REPLICAS,
        compiler_params=params_for(24),
        cost_estimate=cost(24 * count * BLOCK**3, 8 * count * BLOCK * BLOCK),
        name="pull",
    )(place, *drots, q)


def unpack_kernel(place_ref, *refs):
    parts, out_ref, packed = refs[:REPLICAS], refs[-2], refs[-1]
    share = HALF // REPLICAS
    for back, part in enumerate(parts):
        start = pl.multiple_of(lax.rem(place_ref[0] + REPLICAS - back, REPLICAS) * share, share)
        packed[:, pl.ds(start, share), :] = part[...]
    for k in range(packed.shape[0]):
        both = packed[k, :, :HALF]
        upper = jnp.where(triangle(False), both, 0.0)
        lower = jnp.where(triangle(True), both, 0.0)
        side = packed[k, :, HALF:]
        out_ref[k, :HALF, :HALF] = upper - upper.T
        out_ref[k, HALF:, HALF:] = lower - lower.T
        out_ref[k, :HALF, HALF:] = side
        out_ref[k, HALF:, :HALF] = -side.T


def unpack(place, parts, group, out):
    count = parts[0].shape[0]
    more = [] if out is None else [pl.BlockSpec(memory_space=pl.ANY)]
    return pl.pallas_call(
        unpack_kernel,
        grid_spec=pltpu.PrefetchScalarGridSpec(
            num_scalar_prefetch=1,
            grid=(1,),
            in_specs=[whole()] * REPLICAS + more,
            out_specs=pl.BlockSpec((count, BLOCK, BLOCK), lambda i, p: (group, 0, 0)),
            scratch_shapes=[pltpu.VMEM((count, HALF, BLOCK), F32)],
        ),
        out_shape=jax.ShapeDtypeStruct((FACTORS, BLOCK, BLOCK), F32),
        input_output_aliases={} if out is None else {1 + REPLICAS: 0},
        compiler_params=params_for(24),
        cost_estimate=cost(0, 12 * count * BLOCK * BLOCK),
        name="unpack",
    )(place, *parts, *(() if out is None else (out,)))


def turn_dp(value, ahead):
    return lax.ppermute(value, "dp", [(i, (i + ahead) % REPLICAS) for i in range(REPLICAS)])


def summed(place, drots, q, first, scale, out):
    pieces = pull(place, drots, q, first, scale)
    mine = pieces[0]
    for ahead in range(1, REPLICAS):
        mine = mine + turn_dp(pieces[ahead], ahead)
    parts = [mine] + [turn_dp(mine, ahead) for ahead in range(1, REPLICAS)]
    return unpack(place, parts, first // len(drots), out)


def spread(slots):
    rows = lax.broadcasted_iota(jnp.int32, (2 * BLOCK, BLOCK), 0)
    return jnp.where(rows == slots, 1.0, 0.0).astype(BF16)


def times(left, right, contract):
    return lax.dot_general(left, right, (contract, ((), ())), preferred_element_type=F32)


def chain_kernel(first, own_ref, arrived_ref, slots_ref, rot_ref, a_ref, keep_ref, send_ref):
    a = own_ref[...] if first else own_ref[...] + arrived_ref[...]
    a_ref[...] = a
    turned = times(a, rot_ref[0], ((1,), (0,))).astype(BF16)
    both = times(turned, spread(slots_ref[0]), ((1,), (1,))).astype(BF16)
    keep_ref[...] = both[:, :BLOCK]
    send_ref[...] = both[:, BLOCK:]


def chain_step(first, own, arrived, slots, rot, factor):
    tokens = own.shape[0]
    full = pl.BlockSpec((tokens, BLOCK), lambda i: (0, 0))
    shape = jax.ShapeDtypeStruct((tokens, BLOCK), BF16)
    return pl.pallas_call(
        functools.partial(chain_kernel, first),
        grid=(1,),
        out_shape=(shape,) * 3,
        in_specs=[
            full,
            full,
            pl.BlockSpec((1, 1, BLOCK), lambda i: (factor, 0, 0)),
            pl.BlockSpec((1, BLOCK, BLOCK), lambda i: (factor, 0, 0)),
        ],
        out_specs=(full,) * 3,
        compiler_params=params_for(24),
        cost_estimate=cost(6 * tokens * BLOCK * BLOCK, 10 * tokens * BLOCK + 2 * BLOCK * BLOCK),
        name=f"chain{factor}",
    )(own, arrived, slots, rot)


def plain_kernel(units, each, count, start, table_ref, *rest):
    arrays = rest[:count]
    weights = rest[count : count + 2 * each]
    before = rest[count + 2 * each : -2]
    own_ref, sib_ref = rest[-2:]
    tokens = own_ref.shape[0]
    step = pl.program_id(0)

    def load(unit):
        parts = [arrays[i][first : first + size, :] for i, first, size in unit]
        return parts[0] if len(parts) == 1 else jnp.concatenate(parts, axis=0)

    def add(group):
        own = jnp.zeros((tokens, BLOCK), F32)
        sib = jnp.zeros((tokens, BLOCK), F32)
        for i in range(each):
            unit = load(units[group * each + i])
            own = own + times(unit, weights[i][...], ((1,), (1,)))
            sib = sib + times(unit, weights[each + i][...], ((1,), (1,)))
        if group == 0 and start:
            own_ref[...] = own
            sib_ref[...] = sib
        elif group == 0:
            own_ref[...] = before[0][...] + own
            sib_ref[...] = before[1][...] + sib
        else:
            own_ref[...] += own
            sib_ref[...] += sib

    for group in range(len(units) // each):
        pl.when(step == group)(functools.partial(add, group))


def plain_part(table, arrays, units, each, frozen, frozen_sib, sums):
    width = arrays[0].shape[1]
    tokens = sum(size for _, _, size in units[0])
    total = len(units)
    start = sums is None
    count = len(arrays)

    def fixed(array):
        return pl.BlockSpec(array.shape, lambda i, t: (0, 0))

    def own_spec(k):
        return pl.BlockSpec((BLOCK, width), lambda i, t: (0, t[i * each + k]))

    def sib_spec(k):
        return pl.BlockSpec((BLOCK, width), lambda i, t: (0, t[i * each + k]))

    out = pl.BlockSpec((tokens, BLOCK), lambda i, t: (0, 0))
    shape = jax.ShapeDtypeStruct((tokens, BLOCK), F32)
    first = 1 + count + 2 * each
    return pl.pallas_call(
        functools.partial(plain_kernel, units, each, count, start),
        grid_spec=pltpu.PrefetchScalarGridSpec(
            num_scalar_prefetch=1,
            grid=(total // each,),
            in_specs=[fixed(array) for array in arrays]
            + [own_spec(k) for k in range(each)]
            + [sib_spec(k) for k in range(each)]
            + ([] if start else [out, out]),
            out_specs=(out, out),
        ),
        out_shape=(shape, shape),
        input_output_aliases={} if start else {first: 0, first + 1: 1},
        compiler_params=params_for(40),
        cost_estimate=cost(
            4 * total * tokens * width * BLOCK, 4 * total * width * BLOCK + 2 * total * tokens * width
        ),
        name="plain",
    )(table, *arrays, *([frozen] * each), *([frozen_sib] * each), *(() if start else sums))


def dense_kernel(units_ref, frozen_ref, out_ref, total):
    step = pl.program_id(0)

    @pl.when(step == 0)
    def _():
        total[...] = jnp.zeros_like(total)

    each, _, width = units_ref.shape
    part = total[...]
    for i in range(each):
        part = part + times(
            units_ref[i], frozen_ref[:, i * width : (i + 1) * width], ((1,), (1,))
        )
    total[...] = part

    @pl.when(step == pl.num_programs(0) - 1)
    def _():
        out_ref[...] = total[...].astype(BF16)


def dense_plain(units, frozen, each):
    count, tokens, width = units.shape
    return pl.pallas_call(
        dense_kernel,
        grid=(count // each,),
        in_specs=[
            pl.BlockSpec((each, tokens, width), lambda i: (i, 0, 0)),
            pl.BlockSpec((BLOCK, each * width), lambda i: (0, i)),
        ],
        out_specs=pl.BlockSpec((tokens, BLOCK), lambda i: (0, 0)),
        out_shape=jax.ShapeDtypeStruct((tokens, BLOCK), BF16),
        scratch_shapes=[pltpu.VMEM((tokens, BLOCK), F32)],
        compiler_params=params_for(40),
        cost_estimate=cost(
            2 * count * tokens * width * BLOCK, 2 * count * width * (tokens + BLOCK)
        ),
        name="dense",
    )(units, frozen)


def stage_kernel(start, offset, own_ref, other_ref, slots_ref, rot_ref, a_ref, *rest):
    out_ref, drot_ref = rest[-2:]
    pick = spread(slots_ref[0])
    g = times(own_ref[...], pick[:BLOCK], ((1,), (0,)))
    g = (g + times(other_ref[...], pick[BLOCK:], ((1,), (0,)))).astype(BF16)
    out_ref[...] = times(g, rot_ref[0], ((1,), (1,))).astype(out_ref.dtype)
    drot = times(a_ref[offset : offset + g.shape[0], :], g, ((0,), (0,)))
    drot_ref[...] = drot if start else rest[0][...] + drot


def stage(own, other, slots, rot, a, drot, factor, offset):
    tokens = own.shape[0]
    full = pl.BlockSpec((tokens, BLOCK), lambda i: (0, 0))
    square = pl.BlockSpec((BLOCK, BLOCK), lambda i: (0, 0))
    kind = F32 if factor == FACTORS - 1 else BF16
    start = drot is None
    return pl.pallas_call(
        functools.partial(stage_kernel, start, offset),
        grid=(1,),
        out_shape=(
            jax.ShapeDtypeStruct((tokens, BLOCK), kind),
            jax.ShapeDtypeStruct((BLOCK, BLOCK), F32),
        ),
        in_specs=[
            full,
            full,
            pl.BlockSpec((1, 1, BLOCK), lambda i: (factor, 0, 0)),
            pl.BlockSpec((1, BLOCK, BLOCK), lambda i: (factor, 0, 0)),
            pl.BlockSpec(a.shape, lambda i: (0, 0)),
        ]
        + ([] if start else [square]),
        out_specs=(full, square),
        input_output_aliases={} if start else {5: 1},
        compiler_params=params_for(24),
        cost_estimate=cost(8 * tokens * BLOCK * BLOCK, 6 * tokens * BLOCK + 10 * BLOCK * BLOCK),
        name=f"stage{factor}",
    )(own, other, slots, rot, a, *(() if start else (drot,)))


def tensor_route(move):
    route = []
    for x in range(XS):
        for z in range(ZS):
            for c in range(CS):
                tx, tz, tc = move(x, z, c)
                route.append(((x * ZS + z) * CS + c, ((tx % XS) * ZS + tz % ZS) * CS + tc))
    return route


def shift(value, dx=0, dz=0):
    return lax.ppermute(value, "tensor", tensor_route(lambda x, z, c: (x + dx, z + dz, c)))


def swap_core(value):
    return lax.ppermute(value, "tensor", tensor_route(lambda x, z, c: (x, z, 1 - c)))


def partner(value, factor):
    count = XS * ZS * CS
    bit = PAIR_BITS[factor]
    return lax.ppermute(value, "tensor", [(i, i ^ bit) for i in range(count)])


def ring(value, **way):
    (axis, _), = way.items()
    half = value.shape[0] // 2
    low = shift(value, **{axis: 1})
    high = shift(value, **{axis: -1})
    far_low = shift(low[:half], **{axis: 1})
    far_high = shift(high[half:], **{axis: -1})
    return low, high, far_low, far_high


def per_device(inputs, cotangent, weight, params, perms, resid_top):
    activ, grad_out, frozen = inputs[0], cotangent[0], weight[0]
    tokens, rows = activ.shape
    width = grad_out.shape[1]
    position = lax.axis_index("tensor")
    core = position % CS
    z_at = position // CS % ZS
    x_at = position // (CS * ZS)

    order = perms[0]
    slots = jnp.where(order // rows == position, order % rows, rows + order % rows)
    slots = slots.reshape(FACTORS, 1, rows)
    rot, q = cayley(params[0])

    size = tokens // SPLIT
    units_late = lax.all_gather(grad_out[size:], "tensor")
    early = grad_out[:size]
    near = ring(early, dx=1)
    low, high, far_low, far_high = ring(early, dz=1)
    frozen_sib = swap_core(frozen)
    offsets = jnp.array([0, -1, 1, 2], jnp.int32)
    spots = ((x_at + offsets) % XS)[:, None] * ZS + ((z_at + offsets) % ZS)[None, :]

    def table(spots):
        return (spots * CS + core).reshape(-1)

    a = [None] * FACTORS
    keep, arrived = activ, activ
    for factor in range(FACTORS - 1, 0, -1):
        first = factor == FACTORS - 1
        a[factor], keep, send = chain_step(first, keep, arrived, slots, rot, factor)
        arrived = partner(send, factor)
    a[0] = keep + arrived

    half = size // 2
    units = [[(0, 0, size)], [(1, 0, size)], [(2, 0, size)], [(3, 0, half), (4, 0, half)]]
    sums = plain_part(
        table(spots[:, 0]), (early,) + near, units, 2, frozen, frozen_sib, None
    )
    pair = jnp.concatenate([low, high], axis=0)
    left, right, far_left, far_right = ring(pair, dx=1)
    units = [[(x, z * size, size)] for x in range(3) for z in range(2)]
    units += [[(3, 0, size)], [(4, 0, size)]]
    sums = plain_part(
        table(spots[:, 1:3]), (pair, left, right, far_left, far_right), units, 2,
        frozen, frozen_sib, sums,
    )
    last = jnp.concatenate([far_low, far_high], axis=0)
    arrays = (last,) + ring(last, dx=1)
    units = [[(0, 0, size)], [(1, 0, size)], [(2, 0, size)], [(3, 0, half), (4, 0, half)]]
    own, sib = plain_part(table(spots[:, 3]), arrays, units, 2, frozen, frozen_sib, sums)

    drot = [None] * FACTORS
    dx = []
    q_sums = None
    place = lax.axis_index("dp")[None]
    scale = 1.0 / math.sqrt(tokens * REPLICAS)
    for part in range(SPLIT):
        if part == 0:
            h = (own + swap_core(sib)).astype(BF16)
        else:
            h = dense_plain(units_late, frozen, 4)
        for factor in range(FACTORS):
            other = partner(h, factor)
            h, drot[factor] = stage(
                h, other, slots, rot, a[factor], drot[factor], factor, part * size
            )
            if part == SPLIT - 1 and factor % 2 == 1:
                q_sums = summed(
                    place, drot[factor - 1 : factor + 1], q, factor - 1, scale, q_sums
                )
        dx.append(h + lax.ppermute(h, "section", [(1, 0)]))
    resid = (resid_top.astype(F32) + jnp.concatenate(dx, axis=0)).astype(BF16)
    return resid[None], q_sums[None]


def solution(mesh):
    placed = (
        P("section", "dp", "tensor"),
        P("section", "dp", "tensor"),
        P("section", "tensor", None),
        P("section", None, "tensor", None),
        P("section", None, "tensor"),
        P("dp", "tensor"),
    )
    return jax.shard_map(
        per_device,
        mesh=mesh,
        in_specs=placed,
        out_specs=(P("section", "dp", "tensor"), P("section", None, "tensor", None)),
        check_vma=False,
    )
```

```python
import functools
import math

import jax
import jax.numpy as jnp
from jax import lax
from jax.experimental import pallas as pl
from jax.experimental.pallas import tpu as pltpu
from jax.sharding import PartitionSpec as P

BLOCK = 256
FACTORS = 4
HALF = BLOCK // 2
EACH = 5
REPLICAS = 4
XS, ZS, CS = 4, 4, 2
F32, BF16 = jnp.float32, jnp.bfloat16
HIGHEST = lax.Precision.HIGHEST
PAIR_BITS = (16, 8, 4, 2)


def params_for(limit):
    return pltpu.CompilerParams(vmem_limit_bytes=limit << 20)


def whole():
    return pl.BlockSpec(memory_space=pltpu.VMEM)


def cost(flops, moved):
    return pl.CostEstimate(flops=flops, bytes_accessed=moved, transcendentals=0)


def identity():
    rows = lax.broadcasted_iota(jnp.int32, (BLOCK, BLOCK), 0)
    cols = lax.broadcasted_iota(jnp.int32, (BLOCK, BLOCK), 1)
    return (rows == cols).astype(F32)


def low_dot(left, right):
    return jnp.dot(left.astype(BF16), right.astype(BF16), preferred_element_type=F32)


def high_dot(left, right):
    return jnp.dot(left, right, preferred_element_type=F32, precision=HIGHEST)


def cayley_kernel(a_ref, rot_ref, q_ref, s_ref):
    eye = identity()
    for k in range(FACTORS):
        a = a_ref[k]
        skew = a - a.T
        s_ref[k] = skew
        square = low_dot(skew, skew)
        row = jnp.max(jnp.sum(jnp.abs(skew), axis=1))
        row_square = jnp.max(jnp.sum(jnp.abs(square), axis=1))
        top = 1.0 + 1.1 * jnp.minimum(row_square, row * row)
        q_ref[k] = (2.0 / (1.0 + top)) * (eye - skew)

    def phase(dot, limit, most):
        def more(carry):
            return (carry[0] < most) & (carry[1] > limit)

        def step(carry):
            worst = jnp.float32(0)
            errors = []
            for k in range(FACTORS):
                error = eye - (q_ref[k] + dot(s_ref[k], q_ref[k]))
                errors.append(error)
                worst = jnp.maximum(worst, jnp.sum(error * error))
            for k in range(FACTORS):
                q_ref[k] = q_ref[k] + low_dot(q_ref[k], errors[k])
            return carry[0] + 1, worst

        lax.while_loop(more, step, (jnp.int32(0), jnp.float32(3e38)))

    phase(low_dot, 0.25, 24)
    phase(high_dot, 1e-6, 12)
    for k in range(FACTORS):
        rot_ref[k] = (2.0 * q_ref[k] - eye).astype(BF16)


def cayley(blocks):
    shape = (FACTORS, BLOCK, BLOCK)
    return pl.pallas_call(
        cayley_kernel,
        out_shape=(jax.ShapeDtypeStruct(shape, BF16), jax.ShapeDtypeStruct(shape, F32)),
        in_specs=[whole()],
        out_specs=(whole(), whole()),
        scratch_shapes=[pltpu.VMEM(shape, F32)],
        compiler_params=params_for(24),
        cost_estimate=cost(7 * 10**9, 10 * FACTORS * BLOCK * BLOCK),
        name="cayley",
    )(blocks)


def triangle(lower):
    rows = lax.broadcasted_iota(jnp.int32, (HALF, HALF), 0)
    cols = lax.broadcasted_iota(jnp.int32, (HALF, HALF), 1)
    return rows > cols if lower else rows < cols


def pull_kernel(first, scale, q_ref, *refs):
    *lefts, own_ref, send_ref = refs
    each = len(lefts) // own_ref.shape[0]
    for k in range(own_ref.shape[0]):
        a_ref, *rights = lefts[k * each : (k + 1) * each]
        drot = jnp.zeros((BLOCK, BLOCK), F32)
        at = 0
        for right in rights:
            size = right.shape[0]
            drot = drot + times(a_ref[at : at + size, :], right[...], ((0,), (0,)))
            at += size
        q_t = q_ref[first + k].T
        grad = high_dot(high_dot(q_t, drot), q_t) * (-2.0 * scale)
        grad = grad - grad.T
        mixed = jnp.where(triangle(True), grad[HALF:, HALF:], grad[:HALF, :HALF])
        own_ref[k, :, :HALF] = mixed
        own_ref[k, :, HALF:] = grad[:HALF, HALF:]
    send_ref[...] = own_ref[...].astype(BF16)


def pull(q, a, g, first, count, scale):
    shape = (count, HALF, BLOCK)
    lefts = []
    for k in range(first, first + count):
        lefts += [a[k], *g[k]]
    return pl.pallas_call(
        functools.partial(pull_kernel, first, scale),
        out_shape=(jax.ShapeDtypeStruct(shape, F32), jax.ShapeDtypeStruct(shape, BF16)),
        in_specs=[whole()] * (1 + len(lefts)),
        out_specs=(whole(), whole()),
        compiler_params=params_for(24),
        cost_estimate=cost(26 * count * BLOCK**3, 12 * count * BLOCK * BLOCK),
        name="pull",
    )(q, *lefts)


def unpack_kernel(*refs):
    own_ref, others, out_ref = refs[0], refs[1:REPLICAS], refs[-1]
    for k in range(own_ref.shape[0]):
        packed = own_ref[k]
        for other in others:
            packed = packed + other[k].astype(F32)
        both, side = packed[:, :HALF], packed[:, HALF:]
        upper = jnp.where(triangle(False), both, 0.0)
        lower = jnp.where(triangle(True), both, 0.0)
        out_ref[0, k, :HALF, :HALF] = upper - upper.T
        out_ref[0, k, HALF:, HALF:] = lower - lower.T
        out_ref[0, k, :HALF, HALF:] = side
        out_ref[0, k, HALF:, :HALF] = -side.T


def unpack(own, others, group, out):
    count = own.shape[0]
    more = [] if out is None else [pl.BlockSpec(memory_space=pl.ANY)]
    return pl.pallas_call(
        unpack_kernel,
        grid=(1,),
        in_specs=[whole()] * REPLICAS + more,
        out_specs=pl.BlockSpec((1, count, BLOCK, BLOCK), lambda i: (0, group, 0, 0)),
        out_shape=jax.ShapeDtypeStruct((1, FACTORS, BLOCK, BLOCK), F32),
        input_output_aliases={} if out is None else {REPLICAS: 0},
        compiler_params=params_for(24),
        cost_estimate=cost(0, 12 * count * BLOCK * BLOCK),
        name="unpack",
    )(own, *others, *(() if out is None else (out,)))


def turn_dp(value, ahead):
    return lax.ppermute(value, "dp", [(i, (i + ahead) % REPLICAS) for i in range(REPLICAS)])


def spread(slots):
    rows = lax.broadcasted_iota(jnp.int32, (2 * BLOCK, BLOCK), 0)
    return jnp.where(rows == slots, 1.0, 0.0).astype(BF16)


def times(left, right, contract):
    return lax.dot_general(left, right, (contract, ((), ())), preferred_element_type=F32)


def chain_kernel(first, own_ref, arrived_ref, slots_ref, rot_ref, a_ref, keep_ref, send_ref):
    a = own_ref[...] if first else own_ref[...] + arrived_ref[...]
    a_ref[...] = a
    turned = times(a, rot_ref[0], ((1,), (0,))).astype(BF16)
    both = times(turned, spread(slots_ref[0]), ((1,), (1,))).astype(BF16)
    keep_ref[...] = both[:, :BLOCK]
    send_ref[...] = both[:, BLOCK:]


def chain_step(first, own, arrived, slots, rot, factor):
    tokens = own.shape[0]
    full = pl.BlockSpec((tokens, BLOCK), lambda i: (0, 0))
    shape = jax.ShapeDtypeStruct((tokens, BLOCK), BF16)
    return pl.pallas_call(
        functools.partial(chain_kernel, first),
        grid=(1,),
        out_shape=(shape,) * 3,
        in_specs=[
            full,
            full,
            pl.BlockSpec((1, 1, BLOCK), lambda i: (factor, 0, 0)),
            pl.BlockSpec((1, BLOCK, BLOCK), lambda i: (factor, 0, 0)),
        ],
        out_specs=(full,) * 3,
        compiler_params=params_for(24),
        cost_estimate=cost(6 * tokens * BLOCK * BLOCK, 10 * tokens * BLOCK + 2 * BLOCK * BLOCK),
        name=f"chain{factor}",
    )(own, arrived, slots, rot)


def plain_kernel(units, each, count, start, table_ref, *rest):
    arrays = rest[:count]
    weights = rest[count : count + 2 * each]
    before = rest[count + 2 * each : -2]
    own_ref, sib_ref = rest[-2:]
    tokens = own_ref.shape[0]
    step = pl.program_id(0)

    def load(unit):
        parts = [arrays[i][first : first + size, :] for i, first, size in unit]
        return parts[0] if len(parts) == 1 else jnp.concatenate(parts, axis=0)

    def add(group):
        own = jnp.zeros((tokens, BLOCK), F32)
        sib = jnp.zeros((tokens, BLOCK), F32)
        for i in range(each):
            unit = load(units[group * each + i])
            own = own + times(unit, weights[i][...], ((1,), (1,)))
            sib = sib + times(unit, weights[each + i][...], ((1,), (1,)))
        if group == 0 and start:
            own_ref[...] = own
            sib_ref[...] = sib
        elif group == 0:
            own_ref[...] = before[0][...] + own
            sib_ref[...] = before[1][...] + sib
        else:
            own_ref[...] += own
            sib_ref[...] += sib

    for group in range(len(units) // each):
        pl.when(step == group)(functools.partial(add, group))


def plain_part(table, arrays, units, each, early, frozen, frozen_sib, sums):
    width = arrays[0].shape[1]
    tokens = sum(size for _, _, size in units[0])
    total = len(units)
    start = sums is None
    count = len(arrays)

    def fixed(array):
        return pl.BlockSpec(array.shape, lambda i, t: (0, 0))

    def own_spec(k):
        return pl.BlockSpec((BLOCK, width), lambda i, t: (0, t[i * each + k]))

    def sib_spec(k):
        return pl.BlockSpec((BLOCK, width), lambda i, t: (0, t[i * each + k]))

    out = pl.BlockSpec((tokens, BLOCK), lambda i, t: (0, 0))
    shape = jax.ShapeDtypeStruct((tokens, BLOCK), F32)
    first = 1 + count + 2 * each
    return pl.pallas_call(
        functools.partial(plain_kernel, units, each, count, start),
        grid_spec=pltpu.PrefetchScalarGridSpec(
            num_scalar_prefetch=1,
            grid=(total // each,),
            in_specs=[whole() if i < early else fixed(array) for i, array in enumerate(arrays)]
            + [own_spec(k) for k in range(each)]
            + [sib_spec(k) for k in range(each)]
            + ([] if start else [out, out]),
            out_specs=(out, out),
        ),
        out_shape=(shape, shape),
        input_output_aliases={} if start else {first: 0, first + 1: 1},
        compiler_params=params_for(48),
        cost_estimate=cost(
            4 * total * tokens * width * BLOCK, 4 * total * width * BLOCK + 2 * total * tokens * width
        ),
        name="plain",
    )(table, *arrays, *([frozen] * each), *([frozen_sib] * each), *(() if start else sums))


def stage_kernel(own_ref, other_ref, slots_ref, rot_ref, out_ref, g_ref):
    pick = spread(slots_ref[0])
    g = times(own_ref[...], pick[:BLOCK], ((1,), (0,)))
    g = (g + times(other_ref[...], pick[BLOCK:], ((1,), (0,)))).astype(BF16)
    g_ref[...] = g
    out_ref[...] = times(g, rot_ref[0], ((1,), (1,))).astype(out_ref.dtype)


def stage(own, other, slots, rot, factor):
    tokens = own.shape[0]
    full = pl.BlockSpec((tokens, BLOCK), lambda i: (0, 0))
    kind = F32 if factor == FACTORS - 1 else BF16
    return pl.pallas_call(
        stage_kernel,
        grid=(1,),
        out_shape=(
            jax.ShapeDtypeStruct((tokens, BLOCK), kind),
            jax.ShapeDtypeStruct((tokens, BLOCK), BF16),
        ),
        in_specs=[
            full,
            full,
            pl.BlockSpec((1, 1, BLOCK), lambda i: (factor, 0, 0)),
            pl.BlockSpec((1, BLOCK, BLOCK), lambda i: (factor, 0, 0)),
        ],
        out_specs=(full, full),
        compiler_params=params_for(24),
        cost_estimate=cost(6 * tokens * BLOCK * BLOCK, 8 * tokens * BLOCK + 2 * BLOCK * BLOCK),
        name=f"stage{factor}",
    )(own, other, slots, rot)


def tensor_route(move):
    route = []
    for x in range(XS):
        for z in range(ZS):
            for c in range(CS):
                tx, tz, tc = move(x, z, c)
                route.append(((x * ZS + z) * CS + c, ((tx % XS) * ZS + tz % ZS) * CS + tc))
    return route


def shift(value, dx=0, dz=0):
    return lax.ppermute(value, "tensor", tensor_route(lambda x, z, c: (x + dx, z + dz, c)))


def swap_core(value):
    return lax.ppermute(value, "tensor", tensor_route(lambda x, z, c: (x, z, 1 - c)))


def partner(value, factor):
    count = XS * ZS * CS
    bit = PAIR_BITS[factor]
    return lax.ppermute(value, "tensor", [(i, i ^ bit) for i in range(count)])


def exchanged(packed, group, grads):
    mine, sent = packed
    others = [turn_dp(sent, ahead) for ahead in range(1, REPLICAS)]
    return unpack(mine, others, group, grads)


def per_device(inputs, cotangent, weight, params, perms, resid_top):
    activ, grad_out, frozen = inputs[0], cotangent[0], weight[0]
    tokens, rows = activ.shape
    width = grad_out.shape[1]
    position = lax.axis_index("tensor")
    core = position % CS
    z_at = position // CS % ZS
    x_at = position // (CS * ZS)

    order = perms[0]
    slots = jnp.where(order // rows == position, order % rows, rows + order % rows)
    slots = slots.reshape(FACTORS, 1, rows)
    rot, q = cayley(params[0])

    frozen_sib = swap_core(frozen)
    offsets = jnp.array([0, -1, 1, 2], jnp.int32)
    spots = ((x_at + offsets) % XS)[:, None] * ZS + ((z_at + offsets) % ZS)[None, :]

    def table(spots):
        return (spots * CS + core).reshape(-1)

    parts = [spots[:, 0], spots[:, 1:3], spots[:3, 3]]
    all_table = jnp.concatenate([table(part) for part in parts])
    end_table = table(spots[3:, 3])
    together = lax.optimization_barrier
    half = tokens // 2

    def both(value, **way):
        (axis, _), = way.items()
        return shift(value, **{axis: 1}), shift(value, **{axis: -1})

    def paired(first, count):
        return [[(i, 0, half), (i + 1, 0, half)] for i in range(first, first + count, 2)]

    first_half, last_half = grad_out[:half], grad_out[half:]
    low_a, high_a = both(first_half, dz=1)
    near = both(grad_out, dx=1)
    low_a, high_a, near, rot = together((low_a, high_a, near, rot))

    low_a_x, high_a_x = both(low_a, dx=1), both(high_a, dx=1)
    low_b, high_b = both(last_half, dz=1)
    far_a = shift(low_a, dz=1)
    near_far = shift(near[0][:half], dx=1), shift(near[1][half:], dx=-1)
    low_a_x, high_a_x, low_b, high_b, far_a = together(
        (low_a_x, high_a_x, low_b, high_b, far_a)
    )

    corner_a = shift(low_a_x[0], dx=1), shift(high_a_x[1], dx=-1)
    low_b_x, high_b_x = both(low_b, dx=1), both(high_b, dx=1)
    far_b = shift(high_b, dz=-1)
    far_a_x = both(far_a, dx=1)
    near_far, corner_a, low_b_x, high_b_x, far_b = together(
        (near_far, corner_a, low_b_x, high_b_x, far_b)
    )

    corner_b = shift(low_b_x[0], dx=1), shift(high_b_x[1], dx=-1)
    far_b_x = both(far_b, dx=1)
    corner_b, far_a_x, far_b_x = together((corner_b, far_a_x, far_b_x))

    end = shift(far_a_x[0], dx=1), shift(far_b_x[1], dx=-1)
    whole_units = [[(i, 0, tokens)] for i in range(3)] + [[(3, 0, half), (4, 0, half)]]
    arrays = (grad_out, *near, *near_far)
    late = (
        low_a, low_b, high_a, high_b,
        low_a_x[0], low_b_x[0], high_a_x[0], high_b_x[0],
        low_a_x[1], low_b_x[1], high_a_x[1], high_b_x[1],
        corner_a[0], corner_b[0], corner_a[1], corner_b[1],
        far_a, far_b, far_a_x[0], far_b_x[0], far_a_x[1], far_b_x[1],
    )
    sums = plain_part(
        all_table, arrays + late, whole_units + paired(5, len(late)), EACH, 21, frozen, frozen_sib, None
    )
    end, sums = together((end, sums))
    own, sib = plain_part(end_table, end, paired(0, 2), 1, 0, frozen, frozen_sib, sums)
    h = (own + swap_core(sib)).astype(BF16)

    a = [None] * FACTORS
    a[3], keep, send = chain_step(True, activ, activ, slots, rot, 3)
    g = []
    scale = 1.0 / math.sqrt(tokens * REPLICAS)
    for factor in range(3):
        back = FACTORS - 1 - factor
        other, arrived = together((partner(h, factor), partner(send, back)))
        h, used = stage(h, other, slots, rot, factor)
        g.append([used])
        if back > 1:
            a[back - 1], keep, send = chain_step(False, keep, arrived, slots, rot, back - 1)
        else:
            a[0] = keep + arrived
    grads = exchanged(pull(q, a, g, 0, 2, scale), 0, None)
    other, grads = together((partner(h, 3), grads))
    h, used = stage(h, other, slots, rot, 3)
    g.append([used])
    grads = exchanged(pull(q, a, g, 2, 2, scale), 1, grads)
    dx = h + lax.ppermute(h, "section", [(1, 0)])
    resid = (resid_top.astype(F32) + dx).astype(BF16)
    return resid[None], grads


def solution(mesh):
    placed = (
        P("section", "dp", "tensor"),
        P("section", "dp", "tensor"),
        P("section", "tensor", None),
        P("section", None, "tensor", None),
        P("section", None, "tensor"),
        P("dp", "tensor"),
    )
    return jax.shard_map(
        per_device,
        mesh=mesh,
        in_specs=placed,
        out_specs=(P("section", "dp", "tensor"), P("section", None, "tensor", None)),
        check_vma=False,
    )
```

```python
import functools
import math

import jax
import jax.numpy as jnp
from jax import lax
from jax.experimental import pallas as pl
from jax.experimental.pallas import tpu as pltpu
from jax.sharding import PartitionSpec as P

BLOCK = 256
FACTORS = 4
HALF = BLOCK // 2
EACH = 5
REPLICAS = 4
XS, ZS, CS = 4, 4, 2
F32, BF16 = jnp.float32, jnp.bfloat16
HIGHEST = lax.Precision.HIGHEST
PAIR_BITS = (16, 8, 4, 2)


def params_for(limit):
    return pltpu.CompilerParams(vmem_limit_bytes=limit << 20)


def whole():
    return pl.BlockSpec(memory_space=pltpu.VMEM)


def cost(flops, moved):
    return pl.CostEstimate(flops=flops, bytes_accessed=moved, transcendentals=0)


def identity():
    rows = lax.broadcasted_iota(jnp.int32, (BLOCK, BLOCK), 0)
    cols = lax.broadcasted_iota(jnp.int32, (BLOCK, BLOCK), 1)
    return (rows == cols).astype(F32)


def low_dot(left, right):
    return jnp.dot(left.astype(BF16), right.astype(BF16), preferred_element_type=F32)


def high_dot(left, right):
    return jnp.dot(left, right, preferred_element_type=F32, precision=HIGHEST)


def cayley_kernel(a_ref, rot_ref, q_ref, s_ref):
    eye = identity()
    for k in range(FACTORS):
        a = a_ref[k]
        skew = a - a.T
        s_ref[k] = skew
        square = low_dot(skew, skew)
        row = jnp.max(jnp.sum(jnp.abs(skew), axis=1))
        row_square = jnp.max(jnp.sum(jnp.abs(square), axis=1))
        top = 1.0 + 1.1 * jnp.minimum(row_square, row * row)
        q_ref[k] = (2.0 / (1.0 + top)) * (eye - skew)

    def phase(dot, limit, most):
        def more(carry):
            return (carry[0] < most) & (carry[1] > limit)

        def step(carry):
            worst = jnp.float32(0)
            errors = []
            for k in range(FACTORS):
                error = eye - (q_ref[k] + dot(s_ref[k], q_ref[k]))
                errors.append(error)
                worst = jnp.maximum(worst, jnp.sum(error * error))
            for k in range(FACTORS):
                q_ref[k] = q_ref[k] + low_dot(q_ref[k], errors[k])
            return carry[0] + 1, worst

        lax.while_loop(more, step, (jnp.int32(0), jnp.float32(3e38)))

    phase(low_dot, 0.25, 24)
    phase(high_dot, 1e-6, 12)
    for k in range(FACTORS):
        rot_ref[k] = (2.0 * q_ref[k] - eye).astype(BF16)


def cayley(blocks):
    shape = (FACTORS, BLOCK, BLOCK)
    return pl.pallas_call(
        cayley_kernel,
        out_shape=(jax.ShapeDtypeStruct(shape, BF16), jax.ShapeDtypeStruct(shape, F32)),
        in_specs=[whole()],
        out_specs=(whole(), whole()),
        scratch_shapes=[pltpu.VMEM(shape, F32)],
        compiler_params=params_for(24),
        cost_estimate=cost(7 * 10**9, 10 * FACTORS * BLOCK * BLOCK),
        name="cayley",
    )(blocks)


def triangle(lower):
    rows = lax.broadcasted_iota(jnp.int32, (HALF, HALF), 0)
    cols = lax.broadcasted_iota(jnp.int32, (HALF, HALF), 1)
    return rows > cols if lower else rows < cols


def pull_kernel(first, scale, q_ref, *refs):
    *lefts, own_ref, send_ref = refs
    each = len(lefts) // own_ref.shape[0]
    for k in range(own_ref.shape[0]):
        a_ref, *rights = lefts[k * each : (k + 1) * each]
        drot = jnp.zeros((BLOCK, BLOCK), F32)
        at = 0
        for right in rights:
            size = right.shape[0]
            drot = drot + times(a_ref[at : at + size, :], right[...], ((0,), (0,)))
            at += size
        q_t = q_ref[first + k].T
        grad = high_dot(high_dot(q_t, drot), q_t) * (-2.0 * scale)
        grad = grad - grad.T
        mixed = jnp.where(triangle(True), grad[HALF:, HALF:], grad[:HALF, :HALF])
        own_ref[k, :, :HALF] = mixed
        own_ref[k, :, HALF:] = grad[:HALF, HALF:]
    send_ref[...] = own_ref[...].astype(BF16)


def pull(q, a, g, first, count, scale):
    shape = (count, HALF, BLOCK)
    lefts = []
    for k in range(first, first + count):
        lefts += [a[k], *g[k]]
    return pl.pallas_call(
        functools.partial(pull_kernel, first, scale),
        out_shape=(jax.ShapeDtypeStruct(shape, F32), jax.ShapeDtypeStruct(shape, BF16)),
        in_specs=[whole()] * (1 + len(lefts)),
        out_specs=(whole(), whole()),
        compiler_params=params_for(24),
        cost_estimate=cost(26 * count * BLOCK**3, 12 * count * BLOCK * BLOCK),
        name="pull",
    )(q, *lefts)


def unpack_kernel(*refs):
    own_ref, others, out_ref = refs[0], refs[1:REPLICAS], refs[-1]
    for k in range(own_ref.shape[0]):
        packed = own_ref[k]
        for other in others:
            packed = packed + other[k].astype(F32)
        both, side = packed[:, :HALF], packed[:, HALF:]
        upper = jnp.where(triangle(False), both, 0.0)
        lower = jnp.where(triangle(True), both, 0.0)
        out_ref[0, k, :HALF, :HALF] = upper - upper.T
        out_ref[0, k, HALF:, HALF:] = lower - lower.T
        out_ref[0, k, :HALF, HALF:] = side
        out_ref[0, k, HALF:, :HALF] = -side.T


def unpack(own, others, group, out):
    count = own.shape[0]
    more = [] if out is None else [pl.BlockSpec(memory_space=pl.ANY)]
    return pl.pallas_call(
        unpack_kernel,
        grid=(1,),
        in_specs=[whole()] * REPLICAS + more,
        out_specs=pl.BlockSpec((1, count, BLOCK, BLOCK), lambda i: (0, group, 0, 0)),
        out_shape=jax.ShapeDtypeStruct((1, FACTORS, BLOCK, BLOCK), F32),
        input_output_aliases={} if out is None else {REPLICAS: 0},
        compiler_params=params_for(24),
        cost_estimate=cost(0, 12 * count * BLOCK * BLOCK),
        name="unpack",
    )(own, *others, *(() if out is None else (out,)))


def turn_dp(value, ahead):
    return lax.ppermute(value, "dp", [(i, (i + ahead) % REPLICAS) for i in range(REPLICAS)])


def spread(slots):
    rows = lax.broadcasted_iota(jnp.int32, (2 * BLOCK, BLOCK), 0)
    return jnp.where(rows == slots, 1.0, 0.0).astype(BF16)


def times(left, right, contract):
    return lax.dot_general(left, right, (contract, ((), ())), preferred_element_type=F32)


def chain_kernel(first, own_ref, arrived_ref, slots_ref, rot_ref, a_ref, keep_ref, send_ref):
    a = own_ref[...] if first else own_ref[...] + arrived_ref[...]
    a_ref[...] = a
    turned = times(a, rot_ref[0], ((1,), (0,))).astype(BF16)
    both = times(turned, spread(slots_ref[0]), ((1,), (1,))).astype(BF16)
    keep_ref[...] = both[:, :BLOCK]
    send_ref[...] = both[:, BLOCK:]


def chain_step(first, own, arrived, slots, rot, factor):
    tokens = own.shape[0]
    full = pl.BlockSpec((tokens, BLOCK), lambda i: (0, 0))
    shape = jax.ShapeDtypeStruct((tokens, BLOCK), BF16)
    return pl.pallas_call(
        functools.partial(chain_kernel, first),
        grid=(1,),
        out_shape=(shape,) * 3,
        in_specs=[
            full,
            full,
            pl.BlockSpec((1, 1, BLOCK), lambda i: (factor, 0, 0)),
            pl.BlockSpec((1, BLOCK, BLOCK), lambda i: (factor, 0, 0)),
        ],
        out_specs=(full,) * 3,
        compiler_params=params_for(24),
        cost_estimate=cost(6 * tokens * BLOCK * BLOCK, 10 * tokens * BLOCK + 2 * BLOCK * BLOCK),
        name=f"chain{factor}",
    )(own, arrived, slots, rot)


def plain_kernel(units, each, count, start, table_ref, *rest):
    arrays = rest[:count]
    weights = rest[count : count + 2 * each]
    before = rest[count + 2 * each : -2]
    own_ref, sib_ref = rest[-2:]
    tokens = own_ref.shape[0]
    step = pl.program_id(0)

    def load(unit):
        parts = [arrays[i][first : first + size, :] for i, first, size in unit]
        return parts[0] if len(parts) == 1 else jnp.concatenate(parts, axis=0)

    def add(group):
        own = jnp.zeros((tokens, BLOCK), F32)
        sib = jnp.zeros((tokens, BLOCK), F32)
        for i in range(each):
            unit = load(units[group * each + i])
            own = own + times(unit, weights[i][...], ((1,), (1,)))
            sib = sib + times(unit, weights[each + i][...], ((1,), (1,)))
        if group == 0 and start:
            own_ref[...] = own
            sib_ref[...] = sib
        elif group == 0:
            own_ref[...] = before[0][...] + own
            sib_ref[...] = before[1][...] + sib
        else:
            own_ref[...] += own
            sib_ref[...] += sib

    for group in range(len(units) // each):
        pl.when(step == group)(functools.partial(add, group))


def plain_part(table, arrays, units, each, early, frozen, frozen_sib, sums):
    width = arrays[0].shape[1]
    tokens = sum(size for _, _, size in units[0])
    total = len(units)
    start = sums is None
    count = len(arrays)

    def fixed(array):
        return pl.BlockSpec(array.shape, lambda i, t: (0, 0))

    def own_spec(k):
        return pl.BlockSpec((BLOCK, width), lambda i, t: (0, t[i * each + k]))

    def sib_spec(k):
        return pl.BlockSpec((BLOCK, width), lambda i, t: (0, t[i * each + k]))

    out = pl.BlockSpec((tokens, BLOCK), lambda i, t: (0, 0))
    shape = jax.ShapeDtypeStruct((tokens, BLOCK), F32)
    first = 1 + count + 2 * each
    return pl.pallas_call(
        functools.partial(plain_kernel, units, each, count, start),
        grid_spec=pltpu.PrefetchScalarGridSpec(
            num_scalar_prefetch=1,
            grid=(total // each,),
            in_specs=[whole() if i < early else fixed(array) for i, array in enumerate(arrays)]
            + [own_spec(k) for k in range(each)]
            + [sib_spec(k) for k in range(each)]
            + ([] if start else [out, out]),
            out_specs=(out, out),
        ),
        out_shape=(shape, shape),
        input_output_aliases={} if start else {first: 0, first + 1: 1},
        compiler_params=params_for(48),
        cost_estimate=cost(
            4 * total * tokens * width * BLOCK, 4 * total * width * BLOCK + 2 * total * tokens * width
        ),
        name="plain",
    )(table, *arrays, *([frozen] * each), *([frozen_sib] * each), *(() if start else sums))


def stage_kernel(own_ref, other_ref, slots_ref, rot_ref, out_ref, g_ref):
    pick = spread(slots_ref[0])
    g = times(own_ref[...], pick[:BLOCK], ((1,), (0,)))
    g = (g + times(other_ref[...], pick[BLOCK:], ((1,), (0,)))).astype(BF16)
    g_ref[...] = g
    out_ref[...] = times(g, rot_ref[0], ((1,), (1,))).astype(out_ref.dtype)


def stage(own, other, slots, rot, factor):
    tokens = own.shape[0]
    full = pl.BlockSpec((tokens, BLOCK), lambda i: (0, 0))
    kind = F32 if factor == FACTORS - 1 else BF16
    return pl.pallas_call(
        stage_kernel,
        grid=(1,),
        out_shape=(
            jax.ShapeDtypeStruct((tokens, BLOCK), kind),
            jax.ShapeDtypeStruct((tokens, BLOCK), BF16),
        ),
        in_specs=[
            full,
            full,
            pl.BlockSpec((1, 1, BLOCK), lambda i: (factor, 0, 0)),
            pl.BlockSpec((1, BLOCK, BLOCK), lambda i: (factor, 0, 0)),
        ],
        out_specs=(full, full),
        compiler_params=params_for(24),
        cost_estimate=cost(6 * tokens * BLOCK * BLOCK, 8 * tokens * BLOCK + 2 * BLOCK * BLOCK),
        name=f"stage{factor}",
    )(own, other, slots, rot)


def tensor_route(move):
    route = []
    for x in range(XS):
        for z in range(ZS):
            for c in range(CS):
                tx, tz, tc = move(x, z, c)
                route.append(((x * ZS + z) * CS + c, ((tx % XS) * ZS + tz % ZS) * CS + tc))
    return route


def shift(value, dx=0, dz=0):
    return lax.ppermute(value, "tensor", tensor_route(lambda x, z, c: (x + dx, z + dz, c)))


def swap_core(value):
    return lax.ppermute(value, "tensor", tensor_route(lambda x, z, c: (x, z, 1 - c)))


def partner(value, factor):
    count = XS * ZS * CS
    bit = PAIR_BITS[factor]
    return lax.ppermute(value, "tensor", [(i, i ^ bit) for i in range(count)])


def exchanged(packed, group, grads):
    mine, sent = packed
    others = [turn_dp(sent, ahead) for ahead in range(1, REPLICAS)]
    return unpack(mine, others, group, grads)


def per_device(inputs, cotangent, weight, params, perms, resid_top):
    activ, grad_out, frozen = inputs[0], cotangent[0], weight[0]
    tokens, rows = activ.shape
    width = grad_out.shape[1]
    position = lax.axis_index("tensor")
    core = position % CS
    z_at = position // CS % ZS
    x_at = position // (CS * ZS)

    order = perms[0]
    slots = jnp.where(order // rows == position, order % rows, rows + order % rows)
    slots = slots.reshape(FACTORS, 1, rows)
    rot, q = cayley(params[0])

    frozen_sib = swap_core(frozen)
    offsets = jnp.array([0, -1, 1, 2], jnp.int32)
    spots = ((x_at + offsets) % XS)[:, None] * ZS + ((z_at + offsets) % ZS)[None, :]

    def table(spots):
        return (spots * CS + core).reshape(-1)

    together = lax.optimization_barrier
    half = tokens // 2

    def both(value, **way):
        (axis, _), = way.items()
        return shift(value, **{axis: 1}), shift(value, **{axis: -1})

    def paired(first, count):
        return [[(i, 0, half), (i + 1, 0, half)] for i in range(first, first + count, 2)]

    first_half, last_half = grad_out[:half], grad_out[half:]
    low_a, high_a = both(first_half, dz=1)
    near = both(grad_out, dx=1)
    low_a, high_a, near, rot = together((low_a, high_a, near, rot))

    pair_a = jnp.concatenate([low_a, high_a], axis=0)
    pair_a_x = both(pair_a, dx=1)
    low_b, high_b = both(last_half, dz=1)
    near_far = shift(near[0][:half], dx=1), shift(near[1][half:], dx=-1)
    pair_a_x, low_b, high_b, near_far = together((pair_a_x, low_b, high_b, near_far))

    pair_b = jnp.concatenate([low_b, high_b], axis=0)
    pair_b_x = both(pair_b, dx=1)
    corner_a = shift(pair_a_x[0][:half], dx=1), shift(pair_a_x[1][half:], dx=-1)
    far_a, far_b = shift(low_a, dz=1), shift(high_b, dz=-1)
    corner_a, pair_b_x, far_a, far_b = together((corner_a, pair_b_x, far_a, far_b))

    corner_b = shift(pair_b_x[0][:half], dx=1), shift(pair_b_x[1][half:], dx=-1)
    far_a_x, far_b_x = both(far_a, dx=1), both(far_b, dx=1)
    corner_b, far_a_x, far_b_x, activ = together((corner_b, far_a_x, far_b_x, activ))

    end = shift(far_a_x[0], dx=1), shift(far_b_x[1], dx=-1)
    a = [None] * FACTORS
    a[3], keep, send = chain_step(True, activ, activ, slots, rot, 3)
    arrived = partner(send, 3)
    units = [[(i, 0, tokens)] for i in range(3)] + [[(3, 0, half), (4, 0, half)]]
    for at in (0, half):
        units += [[(i, at, half), (i + 1, at, half)] for i in (5, 7, 9)]
        units += [[(11 + at // half, 0, half), (13 + at // half, 0, half)]]
    arrays = (
        grad_out, *near, *near_far,
        pair_a, pair_b, pair_a_x[0], pair_b_x[0], pair_a_x[1], pair_b_x[1],
        *corner_a, *corner_b,
        far_a, far_b, far_a_x[0], far_b_x[0], far_a_x[1], far_b_x[1],
    )
    units += paired(15, 6)
    parts = [spots[:, 0], spots[:, 1], spots[:, 2], spots[:3, 3]]
    all_table = jnp.concatenate([table(part) for part in parts])
    sums = plain_part(all_table, arrays, units, EACH, 15, frozen, frozen_sib, None)
    end, sums, arrived = together((end, sums, arrived))
    own, sib = plain_part(table(spots[3:, 3]), end, paired(0, 2), 1, 0, frozen, frozen_sib, sums)
    h = (own + swap_core(sib)).astype(BF16)
    a[2], keep, send = chain_step(False, keep, arrived, slots, rot, 2)

    g = []
    scale = 1.0 / math.sqrt(tokens * REPLICAS)

    def staged(h, other, factor):
        h, used = stage(h, other, slots, rot, factor)
        g.append([used])
        return h

    arrived = partner(send, 2)
    h = staged(h, partner(h, 0), 0)
    other, arrived = together((partner(h, 1), arrived))
    h = staged(h, other, 1)
    a[1], keep, send = chain_step(False, keep, arrived, slots, rot, 1)
    a[0] = keep + partner(send, 1)
    other, first = together((partner(h, 2), pull(q, a, g, 0, 2, scale)))
    h = staged(h, other, 2)
    other, grads = together((partner(h, 3), exchanged(first, 0, None)))
    h = staged(h, other, 3)
    grads = exchanged(pull(q, a, g, 2, 2, scale), 1, grads)
    dx = h + lax.ppermute(h, "section", [(1, 0)])
    resid = (resid_top.astype(F32) + dx).astype(BF16)
    return resid[None], grads


def solution(mesh):
    placed = (
        P("section", "dp", "tensor"),
        P("section", "dp", "tensor"),
        P("section", "tensor", None),
        P("section", None, "tensor", None),
        P("section", None, "tensor"),
        P("dp", "tensor"),
    )
    return jax.shard_map(
        per_device,
        mesh=mesh,
        in_specs=placed,
        out_specs=(P("section", "dp", "tensor"), P("section", None, "tensor", None)),
        check_vma=False,
    )
```

```python
import functools
import math

import jax
import jax.numpy as jnp
from jax import lax
from jax.experimental import pallas as pl
from jax.experimental.pallas import tpu as pltpu
from jax.sharding import PartitionSpec as P

BLOCK = 256
FACTORS = 4
HALF = BLOCK // 2
EACH = 5
REPLICAS = 4
XS, ZS, CS = 4, 4, 2
F32, BF16 = jnp.float32, jnp.bfloat16
HIGHEST = lax.Precision.HIGHEST
PAIR_BITS = (16, 8, 4, 2)


def params_for(limit):
    return pltpu.CompilerParams(vmem_limit_bytes=limit << 20)


def whole():
    return pl.BlockSpec(memory_space=pltpu.VMEM)


def cost(flops, moved):
    return pl.CostEstimate(flops=flops, bytes_accessed=moved, transcendentals=0)


def identity():
    rows = lax.broadcasted_iota(jnp.int32, (BLOCK, BLOCK), 0)
    cols = lax.broadcasted_iota(jnp.int32, (BLOCK, BLOCK), 1)
    return (rows == cols).astype(F32)


def low_dot(left, right):
    return jnp.dot(left.astype(BF16), right.astype(BF16), preferred_element_type=F32)


def high_dot(left, right):
    return jnp.dot(left, right, preferred_element_type=F32, precision=HIGHEST)


def cayley_kernel(a_ref, rot_ref, q_ref, s_ref):
    eye = identity()
    for k in range(FACTORS):
        a = a_ref[k]
        skew = a - a.T
        s_ref[k] = skew
        square = low_dot(skew, skew)
        row = jnp.max(jnp.sum(jnp.abs(skew), axis=1))
        row_square = jnp.max(jnp.sum(jnp.abs(square), axis=1))
        top = 1.0 + 1.1 * jnp.minimum(row_square, row * row)
        q_ref[k] = (2.0 / (1.0 + top)) * (eye - skew)

    def phase(dot, limit, most):
        def more(carry):
            return (carry[0] < most) & (carry[1] > limit)

        def step(carry):
            worst = jnp.float32(0)
            errors = []
            for k in range(FACTORS):
                error = eye - (q_ref[k] + dot(s_ref[k], q_ref[k]))
                errors.append(error)
                worst = jnp.maximum(worst, jnp.sum(error * error))
            for k in range(FACTORS):
                q_ref[k] = q_ref[k] + low_dot(q_ref[k], errors[k])
            return carry[0] + 1, worst

        lax.while_loop(more, step, (jnp.int32(0), jnp.float32(3e38)))

    phase(low_dot, 0.25, 24)
    phase(high_dot, 1e-6, 12)
    for k in range(FACTORS):
        rot_ref[k] = (2.0 * q_ref[k] - eye).astype(BF16)


def cayley(blocks):
    shape = (FACTORS, BLOCK, BLOCK)
    return pl.pallas_call(
        cayley_kernel,
        out_shape=(jax.ShapeDtypeStruct(shape, BF16), jax.ShapeDtypeStruct(shape, F32)),
        in_specs=[whole()],
        out_specs=(whole(), whole()),
        scratch_shapes=[pltpu.VMEM(shape, F32)],
        compiler_params=params_for(24),
        cost_estimate=cost(7 * 10**9, 10 * FACTORS * BLOCK * BLOCK),
        name="cayley",
    )(blocks)


def triangle(lower):
    rows = lax.broadcasted_iota(jnp.int32, (HALF, HALF), 0)
    cols = lax.broadcasted_iota(jnp.int32, (HALF, HALF), 1)
    return rows > cols if lower else rows < cols


def pull_kernel(first, scale, q_ref, *refs):
    *lefts, own_ref, send_ref = refs
    each = len(lefts) // own_ref.shape[0]
    for k in range(own_ref.shape[0]):
        a_ref, *rights = lefts[k * each : (k + 1) * each]
        drot = jnp.zeros((BLOCK, BLOCK), F32)
        at = 0
        for right in rights:
            size = right.shape[0]
            drot = drot + times(a_ref[at : at + size, :], right[...], ((0,), (0,)))
            at += size
        q_t = q_ref[first + k].T
        grad = high_dot(high_dot(q_t, drot), q_t) * (-2.0 * scale)
        grad = grad - grad.T
        mixed = jnp.where(triangle(True), grad[HALF:, HALF:], grad[:HALF, :HALF])
        own_ref[k, :, :HALF] = mixed
        own_ref[k, :, HALF:] = grad[:HALF, HALF:]
    send_ref[...] = own_ref[...].astype(BF16)


def pull(q, a, g, first, count, scale):
    shape = (count, HALF, BLOCK)
    lefts = []
    for k in range(first, first + count):
        lefts += [a[k], *g[k]]
    return pl.pallas_call(
        functools.partial(pull_kernel, first, scale),
        out_shape=(jax.ShapeDtypeStruct(shape, F32), jax.ShapeDtypeStruct(shape, BF16)),
        in_specs=[whole()] * (1 + len(lefts)),
        out_specs=(whole(), whole()),
        compiler_params=params_for(24),
        cost_estimate=cost(26 * count * BLOCK**3, 12 * count * BLOCK * BLOCK),
        name="pull",
    )(q, *lefts)


def unpack_kernel(*refs):
    own_ref, others, out_ref = refs[0], refs[1:REPLICAS], refs[-1]
    for k in range(own_ref.shape[0]):
        packed = own_ref[k]
        for other in others:
            packed = packed + other[k].astype(F32)
        both, side = packed[:, :HALF], packed[:, HALF:]
        upper = jnp.where(triangle(False), both, 0.0)
        lower = jnp.where(triangle(True), both, 0.0)
        out_ref[0, k, :HALF, :HALF] = upper - upper.T
        out_ref[0, k, HALF:, HALF:] = lower - lower.T
        out_ref[0, k, :HALF, HALF:] = side
        out_ref[0, k, HALF:, :HALF] = -side.T


def unpack(own, others, group, out):
    count = own.shape[0]
    more = [] if out is None else [pl.BlockSpec(memory_space=pl.ANY)]
    return pl.pallas_call(
        unpack_kernel,
        grid=(1,),
        in_specs=[whole()] * REPLICAS + more,
        out_specs=pl.BlockSpec((1, count, BLOCK, BLOCK), lambda i: (0, group, 0, 0)),
        out_shape=jax.ShapeDtypeStruct((1, FACTORS, BLOCK, BLOCK), F32),
        input_output_aliases={} if out is None else {REPLICAS: 0},
        compiler_params=params_for(24),
        cost_estimate=cost(0, 12 * count * BLOCK * BLOCK),
        name="unpack",
    )(own, *others, *(() if out is None else (out,)))


def turn_dp(value, ahead):
    return lax.ppermute(value, "dp", [(i, (i + ahead) % REPLICAS) for i in range(REPLICAS)])


def spread(slots):
    rows = lax.broadcasted_iota(jnp.int32, (2 * BLOCK, BLOCK), 0)
    return jnp.where(rows == slots, 1.0, 0.0).astype(BF16)


def times(left, right, contract):
    return lax.dot_general(left, right, (contract, ((), ())), preferred_element_type=F32)


def chain_kernel(first, own_ref, arrived_ref, slots_ref, rot_ref, a_ref, keep_ref, send_ref):
    a = own_ref[...] if first else own_ref[...] + arrived_ref[...]
    a_ref[...] = a
    turned = times(a, rot_ref[0], ((1,), (0,))).astype(BF16)
    both = times(turned, spread(slots_ref[0]), ((1,), (1,))).astype(BF16)
    keep_ref[...] = both[:, :BLOCK]
    send_ref[...] = both[:, BLOCK:]


def chain_step(first, own, arrived, slots, rot, factor):
    tokens = own.shape[0]
    full = pl.BlockSpec((tokens, BLOCK), lambda i: (0, 0))
    shape = jax.ShapeDtypeStruct((tokens, BLOCK), BF16)
    return pl.pallas_call(
        functools.partial(chain_kernel, first),
        grid=(1,),
        out_shape=(shape,) * 3,
        in_specs=[
            full,
            full,
            pl.BlockSpec((1, 1, BLOCK), lambda i: (factor, 0, 0)),
            pl.BlockSpec((1, BLOCK, BLOCK), lambda i: (factor, 0, 0)),
        ],
        out_specs=(full,) * 3,
        compiler_params=params_for(24),
        cost_estimate=cost(6 * tokens * BLOCK * BLOCK, 10 * tokens * BLOCK + 2 * BLOCK * BLOCK),
        name=f"chain{factor}",
    )(own, arrived, slots, rot)


def plain_kernel(units, each, count, start, table_ref, *rest):
    arrays = rest[:count]
    weights = rest[count : count + 2 * each]
    before = rest[count + 2 * each : -2]
    own_ref, sib_ref = rest[-2:]
    tokens = own_ref.shape[0]
    step = pl.program_id(0)

    def load(unit):
        parts = [arrays[i][first : first + size, :] for i, first, size in unit]
        return parts[0] if len(parts) == 1 else jnp.concatenate(parts, axis=0)

    def add(group):
        own = jnp.zeros((tokens, BLOCK), F32)
        sib = jnp.zeros((tokens, BLOCK), F32)
        for i in range(each):
            unit = load(units[group * each + i])
            own = own + times(unit, weights[i][...], ((1,), (1,)))
            sib = sib + times(unit, weights[each + i][...], ((1,), (1,)))
        if group == 0 and start:
            own_ref[...] = own
            sib_ref[...] = sib
        elif group == 0:
            own_ref[...] = before[0][...] + own
            sib_ref[...] = before[1][...] + sib
        else:
            own_ref[...] += own
            sib_ref[...] += sib

    for group in range(len(units) // each):
        pl.when(step == group)(functools.partial(add, group))


def plain_part(table, arrays, units, each, early, frozen, frozen_sib, sums):
    width = arrays[0].shape[1]
    tokens = sum(size for _, _, size in units[0])
    total = len(units)
    start = sums is None
    count = len(arrays)

    def fixed(array):
        return pl.BlockSpec(array.shape, lambda i, t: (0, 0))

    def own_spec(k):
        return pl.BlockSpec((BLOCK, width), lambda i, t: (0, t[i * each + k]))

    def sib_spec(k):
        return pl.BlockSpec((BLOCK, width), lambda i, t: (0, t[i * each + k]))

    out = pl.BlockSpec((tokens, BLOCK), lambda i, t: (0, 0))
    shape = jax.ShapeDtypeStruct((tokens, BLOCK), F32)
    first = 1 + count + 2 * each
    return pl.pallas_call(
        functools.partial(plain_kernel, units, each, count, start),
        grid_spec=pltpu.PrefetchScalarGridSpec(
            num_scalar_prefetch=1,
            grid=(total // each,),
            in_specs=[whole() if i < early else fixed(array) for i, array in enumerate(arrays)]
            + [own_spec(k) for k in range(each)]
            + [sib_spec(k) for k in range(each)]
            + ([] if start else [out, out]),
            out_specs=(out, out),
        ),
        out_shape=(shape, shape),
        input_output_aliases={} if start else {first: 0, first + 1: 1},
        compiler_params=params_for(48),
        cost_estimate=cost(
            4 * total * tokens * width * BLOCK, 4 * total * width * BLOCK + 2 * total * tokens * width
        ),
        name="plain",
    )(table, *arrays, *([frozen] * each), *([frozen_sib] * each), *(() if start else sums))


def stage_kernel(own_ref, other_ref, slots_ref, rot_ref, out_ref, g_ref):
    pick = spread(slots_ref[0])
    g = times(own_ref[...], pick[:BLOCK], ((1,), (0,)))
    g = (g + times(other_ref[...], pick[BLOCK:], ((1,), (0,)))).astype(BF16)
    g_ref[...] = g
    out_ref[...] = times(g, rot_ref[0], ((1,), (1,))).astype(out_ref.dtype)


def stage(own, other, slots, rot, factor):
    tokens = own.shape[0]
    full = pl.BlockSpec((tokens, BLOCK), lambda i: (0, 0))
    kind = F32 if factor == FACTORS - 1 else BF16
    return pl.pallas_call(
        stage_kernel,
        grid=(1,),
        out_shape=(
            jax.ShapeDtypeStruct((tokens, BLOCK), kind),
            jax.ShapeDtypeStruct((tokens, BLOCK), BF16),
        ),
        in_specs=[
            full,
            full,
            pl.BlockSpec((1, 1, BLOCK), lambda i: (factor, 0, 0)),
            pl.BlockSpec((1, BLOCK, BLOCK), lambda i: (factor, 0, 0)),
        ],
        out_specs=(full, full),
        compiler_params=params_for(24),
        cost_estimate=cost(6 * tokens * BLOCK * BLOCK, 8 * tokens * BLOCK + 2 * BLOCK * BLOCK),
        name=f"stage{factor}",
    )(own, other, slots, rot)


def tensor_route(move):
    route = []
    for x in range(XS):
        for z in range(ZS):
            for c in range(CS):
                tx, tz, tc = move(x, z, c)
                route.append(((x * ZS + z) * CS + c, ((tx % XS) * ZS + tz % ZS) * CS + tc))
    return route


def shift(value, dx=0, dz=0):
    return lax.ppermute(value, "tensor", tensor_route(lambda x, z, c: (x + dx, z + dz, c)))


def swap_core(value):
    return lax.ppermute(value, "tensor", tensor_route(lambda x, z, c: (x, z, 1 - c)))


def partner(value, factor):
    count = XS * ZS * CS
    bit = PAIR_BITS[factor]
    return lax.ppermute(value, "tensor", [(i, i ^ bit) for i in range(count)])


def exchanged(packed, group, grads):
    mine, sent = packed
    others = [turn_dp(sent, ahead) for ahead in range(1, REPLICAS)]
    return unpack(mine, others, group, grads)


def per_device(inputs, cotangent, weight, params, perms, resid_top):
    activ, grad_out, frozen = inputs[0], cotangent[0], weight[0]
    tokens, rows = activ.shape
    width = grad_out.shape[1]
    position = lax.axis_index("tensor")
    core = position % CS
    z_at = position // CS % ZS
    x_at = position // (CS * ZS)

    order = perms[0]
    slots = jnp.where(order // rows == position, order % rows, rows + order % rows)
    slots = slots.reshape(FACTORS, 1, rows)
    rot, q = cayley(params[0])

    frozen_sib = swap_core(frozen)
    offsets = jnp.array([0, -1, 1, 2], jnp.int32)
    spots = ((x_at + offsets) % XS)[:, None] * ZS + ((z_at + offsets) % ZS)[None, :]

    def table(spots):
        return (spots * CS + core).reshape(-1)

    together = lax.optimization_barrier
    half = tokens // 2

    def both(value, **way):
        (axis, _), = way.items()
        return shift(value, **{axis: 1}), shift(value, **{axis: -1})

    def paired(first, count):
        return [[(i, 0, half), (i + 1, 0, half)] for i in range(first, first + count, 2)]

    first_half, last_half = grad_out[:half], grad_out[half:]
    low_a, high_a = both(first_half, dz=1)
    near = both(grad_out, dx=1)
    low_a, high_a, near, rot = together((low_a, high_a, near, rot))

    pair_a = jnp.concatenate([low_a, high_a], axis=0)
    pair_a_x = both(pair_a, dx=1)
    low_b, high_b = both(last_half, dz=1)
    near_far = shift(near[0][:half], dx=1), shift(near[1][half:], dx=-1)
    pair_a_x, low_b, high_b, near_far = together((pair_a_x, low_b, high_b, near_far))

    pair_b = jnp.concatenate([low_b, high_b], axis=0)
    pair_b_x = both(pair_b, dx=1)
    corner_a = shift(pair_a_x[0][:half], dx=1), shift(pair_a_x[1][half:], dx=-1)
    far_a, far_b = shift(low_a, dz=1), shift(high_b, dz=-1)
    corner_a, pair_b_x, far_a, far_b, activ = together(
        (corner_a, pair_b_x, far_a, far_b, activ)
    )

    corner_b = shift(pair_b_x[0][:half], dx=1), shift(pair_b_x[1][half:], dx=-1)
    far_a_x, far_b_x = both(far_a, dx=1), both(far_b, dx=1)
    a = [None] * FACTORS
    a[3], keep, send = chain_step(True, activ, activ, slots, rot, 3)
    arrived = partner(send, 3)
    corner_b, far_a_x, far_b_x, keep = together((corner_b, far_a_x, far_b_x, keep))

    end = shift(far_a_x[0], dx=1), shift(far_b_x[1], dx=-1)
    units = [[(i, 0, tokens)] for i in range(3)] + [[(3, 0, half), (4, 0, half)]]
    for at in (0, half):
        units += [[(i, at, half), (i + 1, at, half)] for i in (5, 7, 9)]
        units += [[(11 + at // half, 0, half), (13 + at // half, 0, half)]]
    arrays = (
        grad_out, *near, *near_far,
        pair_a, pair_b, pair_a_x[0], pair_b_x[0], pair_a_x[1], pair_b_x[1],
        *corner_a, *corner_b,
        far_a, far_b, far_a_x[0], far_b_x[0], far_a_x[1], far_b_x[1],
    )
    units += paired(15, 6)
    parts = [spots[:, 0], spots[:, 1], spots[:, 2], spots[:3, 3]]
    all_table = jnp.concatenate([table(part) for part in parts])
    sums = plain_part(all_table, arrays, units, EACH, 15, frozen, frozen_sib, None)
    end, sums, arrived = together((end, sums, arrived))
    own, sib = plain_part(table(spots[3:, 3]), end, paired(0, 2), 1, 0, frozen, frozen_sib, sums)
    h = (own + swap_core(sib)).astype(BF16)
    a[2], keep, send = chain_step(False, keep, arrived, slots, rot, 2)

    g = []
    scale = 1.0 / math.sqrt(tokens * REPLICAS)

    def staged(h, other, factor):
        h, used = stage(h, other, slots, rot, factor)
        g.append([used])
        return h

    arrived = partner(send, 2)
    h = staged(h, partner(h, 0), 0)
    other, arrived = together((partner(h, 1), arrived))
    h = staged(h, other, 1)
    a[1], keep, send = chain_step(False, keep, arrived, slots, rot, 1)
    a[0] = keep + partner(send, 1)
    other, first = together((partner(h, 2), pull(q, a, g, 0, 2, scale)))
    h = staged(h, other, 2)
    other, grads = together((partner(h, 3), exchanged(first, 0, None)))
    h = staged(h, other, 3)
    grads = exchanged(pull(q, a, g, 2, 2, scale), 1, grads)
    dx = h + lax.ppermute(h, "section", [(1, 0)])
    resid = (resid_top.astype(F32) + dx).astype(BF16)
    return resid[None], grads


def solution(mesh):
    placed = (
        P("section", "dp", "tensor"),
        P("section", "dp", "tensor"),
        P("section", "tensor", None),
        P("section", None, "tensor", None),
        P("section", None, "tensor"),
        P("dp", "tensor"),
    )
    return jax.shard_map(
        per_device,
        mesh=mesh,
        in_specs=placed,
        out_specs=(P("section", "dp", "tensor"), P("section", None, "tensor", None)),
        check_vma=False,
    )
```
